512 devices in a mesh: dp: 16 (over z, core), expert: 32 (over y, x).
Axes of the slice: x: 4, y: 8, z: 8, core: 2. Of those that a mesh axis runs over, the one named last changes fastest.
Arguments:
- tokens: bfloat16 [4096, 2048], P(('dp', 'expert')), may hold values from -6 to 6
- grad_out: bfloat16 [4096, 2048], P(('dp', 'expert')), may hold values from -6 to 6
- gate_weights: bfloat16 [4096, 4], P(('dp', 'expert')), may hold values from 0.049804688 to 0.59765625
- expert_ids: int32 [4096, 4], P(('dp', 'expert')), may hold values from 0 to 31, all different within a row; in each aligned block of 8 rows (0 to 7, 8 to 15, ...) at most 2 rows name the same one
- w_gate: bfloat16 [32, 2048, 2048], P('expert', None, 'dp'), may hold values from -0.125 to 0.125
- w_up: bfloat16 [32, 2048, 2048], P('expert', None, 'dp'), may hold values from -0.125 to 0.125
- w_down: bfloat16 [32, 2048, 2048], P('expert', 'dp'), may hold values from -0.125 to 0.125
Outputs:
- grad_tokens: bfloat16 [4096, 2048], P(('dp', 'expert'))
- grad_w_gate: float32 [32, 2048, 2048], P('expert', None, 'dp')
- grad_w_up: float32 [32, 2048, 2048], P('expert', None, 'dp')
- grad_w_down: float32 [32, 2048, 2048], P('expert', 'dp')
The draws below stay inside these ranges and needn't reach their ends.
Inputs may be any that keep to these rules, and one draw needn't show every extreme that they name: `expert_ids`: each row names 4 different experts. Among the 8 rows of one device no expert is named more than 2 times, and in every draw some expert is named exactly 2 times by the rows of some device.
All inputs are finite; a program needn't handle non-finite values.
Results may differ from the reference program's by a relative error of at most 0.024.
Values may be sent and summed in bfloat16 or wider, within the bound.
A program may use at most 64 MiB of HBM per device.

```python
import math
import jax
import jax.numpy as jnp
import numpy as np
from jax import lax

D = 2048
FF = 2048
TOP = 4
TOK_DEV = 8
EXPERTS = 32
CAP = 2
TOKENS = 4096
N_DP = 16


def level_of(rng, extent, cuts, least, high):
    def one(axis_at, blocks):
        draws = jax.random.uniform(jax.random.fold_in(jax.random.fold_in(rng, 6), axis_at), (blocks,), jnp.float32, least / len(cuts), high / len(cuts))
        return jnp.repeat(jnp.exp(draws), extent[axis_at] // blocks).reshape((-1,) + (1,) * (len(extent) - axis_at - 1))

    loudness = one(*cuts[0])
    for cut in cuts[1:]:
        loudness = loudness * one(*cut)
    return loudness


def deal_out(stream_key, own, number, rows, count, top, bound, slope):
    order = jax.random.permutation(stream_key, count)
    heavy_load, common = load_shares(count, rows * top, bound, slope, True), load_shares(count, rows * top, bound, slope, False)
    places = jnp.arange(count)

    def named(sizes, turn):
        used = int((sizes > 0).sum())
        fixed = max(1, used // 4)
        shifted = fixed + (places - fixed + turn * (used - fixed)) % max(1, count - fixed)
        return jnp.zeros((count,), jnp.int32).at[order[jnp.where(places < fixed, places, shifted)]].set(jnp.asarray(sizes, jnp.int32))

    sizes = jnp.where(number % 4 == 0, named(heavy_load, number // 4), named(common, number - number // 4 - 1))
    mixed = jax.random.permutation(jax.random.fold_in(own, 3), count)
    source_of, receiver = mixed[0:count // 2 * 2:2], mixed[1:count // 2 * 2:2]
    room = jnp.minimum(sizes[source_of] - 1, bound - sizes[receiver]) // 2
    room = jnp.where((source_of == order[0]) | (receiver == order[0]) | (sizes[receiver] == 0), 0, jnp.maximum(room, 0))
    shifted = jax.random.randint(jax.random.fold_in(own, 4), (count // 2,), 0, 1 << 20) % (room + 1)
    sizes = sizes.at[source_of].add(-shifted).at[receiver].add(shifted)
    items = jnp.searchsorted(jnp.cumsum(sizes), jnp.arange(rows * top), side="right").astype(jnp.int32)
    table = items.reshape(top, rows).T
    table = table[jax.random.permutation(jax.random.fold_in(own, 1), rows)]
    turn = jax.random.randint(jax.random.fold_in(own, 2), (rows, 1), 0, top)
    return jnp.take_along_axis(table, (jnp.arange(top)[None, :] + turn) % top, axis=1)


def load_shares(number_of, total, reach, skew, full):
    loads = [(1 << 20) // math.isqrt(standing ** skew) + 1 for standing in range(1, number_of + 1)]
    largest = reach if full else min(reach, max(-(-total // number_of), total * loads[0] // sum(loads)))
    least = 1 if total - largest >= number_of - 1 else 0
    holding, rest = [largest] + [least] * (number_of - 1), total - largest - least * (number_of - 1)
    while rest > 0:
        candidates = [i for i in range(1, number_of) if holding[i] < largest] or [i for i in range(1, number_of) if holding[i] < reach]
        whole, budget = sum([loads[i] for i in candidates]), rest
        for i in candidates:
            extra = min(reach - holding[i], max(1, budget * loads[i] // whole), rest)
            holding[i] = holding[i] + extra
            rest = rest - extra
    return np.array(holding)


def gaussian(key, extent, spread, reach, shards=(), kind=jnp.bfloat16):
    result = jax.random.normal(key, extent, jnp.float32) * spread
    if len(shards) > 0:
        result = level_of(key, extent, shards, -0.22, 0.18) * result
    return jnp.clip(result, min=-reach, max=reach).astype(kind)


def setup_inputs(seed: int = 0) -> dict:
    seeds = jax.random.split(jax.random.key(seed), 8)
    tokens = gaussian(seeds[0], (TOKENS, D), 1.0, 6.0, ((0, 512),))
    grad_out = gaussian(seeds[1], (TOKENS, D), 1.0, 6.0, ((0, 512),))
    gate_weights = jnp.clip(0.049804688 + 0.54785156 * jax.random.uniform(seeds[2], (TOKENS, TOP), jnp.float32) ** level_of(seeds[2], (TOKENS, TOP), ((0, 512),), -0.2, 0.2), 0.049804688, 0.59765625).astype(jnp.bfloat16)
    expert_ids_keys = jax.random.split(jax.random.fold_in(seeds[3], 1), TOKENS // TOK_DEV)
    expert_ids_turns = jax.random.permutation(jax.random.fold_in(seeds[3], 3), TOKENS // TOK_DEV)
    expert_ids = jax.vmap(lambda own, number: deal_out(jax.random.fold_in(seeds[3], 2), own, number, TOK_DEV, EXPERTS, TOP, CAP, 2))(expert_ids_keys, expert_ids_turns).reshape((TOKENS, TOP))
    w_gate = gaussian(seeds[4], (EXPERTS, D, FF), D ** -0.5, 0.125, ((0, 32), (2, 16)))
    w_up = gaussian(seeds[5], (EXPERTS, D, FF), D ** -0.5, 0.125, ((0, 32), (2, 16)))
    w_down = gaussian(seeds[6], (EXPERTS, FF, D), FF ** -0.5, 0.125, ((0, 32), (1, 16)))
    return dict(tokens=tokens, grad_out=grad_out, gate_weights=gate_weights, expert_ids=expert_ids, w_gate=w_gate, w_up=w_up, w_down=w_down)


def expert_backward(operands):
    routed_rows, scaled, gate_mat, up_mat, down_mat = operands
    gate_pre = jnp.dot(routed_rows, gate_mat, preferred_element_type=jnp.float32)
    up_pre = jnp.dot(routed_rows, up_mat, preferred_element_type=jnp.float32)
    logistic = jax.nn.sigmoid(gate_pre)
    activated = gate_pre * logistic
    hidden = (activated * up_pre).astype(jnp.bfloat16)
    grad_hidden = jnp.dot(scaled, down_mat.T, preferred_element_type=jnp.float32)
    grad_up = (grad_hidden * activated).astype(jnp.bfloat16)
    grad_gate = (grad_hidden * up_pre * (logistic * (1.0 + gate_pre * (1.0 - logistic)))).astype(jnp.bfloat16)
    gate_grad = jnp.dot(routed_rows.T, grad_gate, preferred_element_type=jnp.float32)
    up_grad = jnp.dot(routed_rows.T, grad_up, preferred_element_type=jnp.float32)
    down_grad = jnp.dot(hidden.T, scaled, preferred_element_type=jnp.float32)
    row_count = routed_rows.shape[0]
    block_width = FF // N_DP
    hidden_grads = jnp.concatenate([grad_gate.reshape(row_count, N_DP, block_width), grad_up.reshape(row_count, N_DP, block_width)], axis=2).astype(jnp.float32)
    stacked = jnp.concatenate([gate_mat.reshape(D, N_DP, block_width), up_mat.reshape(D, N_DP, block_width)], axis=2).astype(jnp.float32)
    block_sums = jnp.einsum("rbh,dbh->rbd", hidden_grads, stacked, precision=lax.Precision.HIGHEST)
    rounded = lax.optimization_barrier(block_sums.astype(jnp.bfloat16)).astype(jnp.float32)
    assign_grad = jnp.sum(rounded, axis=1).astype(jnp.bfloat16)
    return assign_grad, gate_grad, up_grad, down_grad


def reference(tokens, grad_out, gate_weights, expert_ids, w_gate, w_up, w_down):
    device_count = TOKENS // TOK_DEV
    slots_total = device_count * CAP
    per_device = TOK_DEV * TOP
    flat_ids = expert_ids.reshape(device_count, per_device)
    position = jnp.arange(per_device, dtype=jnp.int32)
    earlier = (flat_ids[:, None, :] == flat_ids[:, :, None]) & (position[None, None, :] < position[None, :, None])
    rank_of = jnp.sum(earlier.astype(jnp.int32), axis=2)
    device_of = jnp.arange(device_count, dtype=jnp.int32)[:, None]
    places = (flat_ids * slots_total + device_of * CAP + rank_of).reshape(-1).astype(jnp.int32)
    token_of = (jnp.arange(TOKENS * TOP, dtype=jnp.int32) // TOP).astype(jnp.int32)
    holder = jnp.full((EXPERTS * slots_total,), TOKENS, jnp.int32).at[places].set(token_of)
    scale_of = jnp.zeros((EXPERTS * slots_total,), jnp.float32).at[places].set(gate_weights.reshape(-1).astype(jnp.float32))
    padded_tokens = jnp.concatenate([tokens, jnp.zeros((1, D), tokens.dtype)], axis=0)
    padded_grads = jnp.concatenate([grad_out, jnp.zeros((1, D), grad_out.dtype)], axis=0)
    routed_rows = padded_tokens[holder].reshape(EXPERTS, slots_total, D)
    scaled = (scale_of[:, None] * padded_grads[holder].astype(jnp.float32)).astype(jnp.bfloat16).reshape(EXPERTS, slots_total, D)
    assign_all, gate_grads, up_grads, down_grads = lax.map(expert_backward, (routed_rows, scaled, w_gate, w_up, w_down))
    per_assign = assign_all.reshape(EXPERTS * slots_total, D)[places]
    grad_tokens = jnp.sum(per_assign.reshape(TOKENS, TOP, D).astype(jnp.float32), axis=1).astype(jnp.bfloat16)
    return grad_tokens, gate_grads, up_grads, down_grads
```

```python
import jax
import jax.numpy as jnp
from jax import lax
from jax.experimental import pallas as pl
from jax.experimental.pallas import tpu as pltpu
from jax.sharding import PartitionSpec as P

NZ, NY, NX = 8, 8, 4
WIDTH, UNITS = 2048, 128
HALF = WIDTH // 2
F32, BF16 = jnp.float32, jnp.bfloat16
ROWS_T = (((0,), (0,)), ((), ()))
COLS_T = (((1,), (1,)), ((), ()))


def dot(a, b, dims=(((1,), (0,)), ((), ()))):
    return lax.dot_general(a, b, dims, preferred_element_type=F32)


def kernel(
    tok, gout, gw, ids, wg_hbm, wu_hbm, wd_hbm,
    gtok, gwg, gwu, gwd,
    wgu, wd, inf, tyx, tyg, xs, gs, xall, gall, szall, hg, hi, pb, pr, qs, qr, ts, tr, fs, fr,
    w_sem, y_send, y_recv, x_send, x_recv, i_send, i_recv, ring_send, ring_recv,
    sib_send, sib_recv, p_send, p_recv, q_send, q_recv, t_send, t_recv, f_send, f_recv,
):
    dp, ex = lax.axis_index("dp"), lax.axis_index("expert")
    z, c = dp // 2, lax.rem(dp, 2)
    y, x = ex // NX, lax.rem(ex, NX)

    def at_z(k):
        return {"dp": lax.rem(z + k + NZ, NZ) * 2 + c, "expert": ex}

    def at_y(k):
        return {"dp": dp, "expert": lax.rem(y + k, NY) * NX + x}

    def at_x(k):
        return {"dp": dp, "expert": y * NX + lax.rem(x + k, NX)}

    sibling = {"dp": z * 2 + 1 - c, "expert": ex}

    def send(src, dst, ssem, rsem, where):
        copy = pltpu.make_async_remote_copy(
            src_ref=src, dst_ref=dst, send_sem=ssem, recv_sem=rsem,
            device_id=where, device_id_type=pl.DeviceIdType.MESH,
        )
        copy.start()

    def wait(ref, sem):
        pltpu.make_async_copy(ref, ref, sem).wait()

    loads = [
        pltpu.make_async_copy(wg_hbm.at[0], wgu.at[:, pl.ds(0, UNITS)], w_sem.at[0]),
        pltpu.make_async_copy(wu_hbm.at[0], wgu.at[:, pl.ds(UNITS, UNITS)], w_sem.at[1]),
        pltpu.make_async_copy(wd_hbm.at[0], wd, w_sem.at[2]),
    ]
    for load in loads:
        load.start()

    barrier = pltpu.get_barrier_semaphore()
    partners = [at_y(k) for k in range(1, NY)] + [at_x(k) for k in range(1, NX)]
    partners += [at_z(k) for k in range(1, NZ)] + [sibling]
    for partner in partners:
        pl.semaphore_signal(barrier, inc=1, device_id=partner, device_id_type=pl.DeviceIdType.MESH)

    lane = lax.broadcasted_iota(jnp.int32, (8, 128), 1)
    info = jnp.zeros((8, 128), F32)
    for k in range(4):
        info = info + jnp.where(lane == k, ids[:, k : k + 1].astype(F32), 0.0)
        info = info + jnp.where(lane == 4 + k, gw[:, k : k + 1].astype(F32), 0.0)
    inf[y] = jnp.concatenate([info, info], axis=0).astype(BF16)
    t32 = tok[...].astype(F32)
    tyx[y] = jnp.concatenate([t32[:, :HALF], t32[:, HALF:]], axis=0).astype(BF16)
    g32 = gout[...].astype(F32)
    tyg[y] = jnp.concatenate([g32[:, :HALF], g32[:, HALF:]], axis=0).astype(BF16)

    pl.semaphore_wait(barrier, len(partners))

    for n, ref in enumerate((inf, tyx, tyg)):
        for k in range(1, NY):
            send(ref.at[y], ref.at[y], y_send.at[n], y_recv.at[n], at_y(k))

    wait(inf.at[pl.ds(0, NY - 1)], y_recv.at[0])
    table = inf[...].reshape(128, 128).astype(F32)
    r = lax.broadcasted_iota(jnp.int32, (128, 128), 0)
    l = lax.broadcasted_iota(jnp.int32, (128, 128), 1)
    same = ((r // 8) % 2 == l // 64) & (r // 16 == (l // 2) % 8)
    expert = (y * NX + (l // 16) % 4).astype(F32)
    named = jnp.zeros((128, 128), F32)
    weight = jnp.zeros((128, 128), F32)
    for k in range(4):
        match = jnp.where(same & (table[:, k : k + 1] == expert), 1.0, 0.0)
        named = named + match
        weight = weight + match * table[:, 4 + k : 5 + k]
    before = jnp.where((r // 8 == l // 8) & (l < r), 1.0, 0.0).astype(BF16)
    rank = dot(before, named.astype(BF16))
    chosen = jnp.where(rank == (l % 2).astype(F32), named, 0.0)
    member = chosen.astype(BF16)
    weighted = (chosen * weight).astype(BF16)
    szall[z] = member
    for k in range(1, NZ):
        send(szall.at[z], szall.at[z], i_send, i_recv, at_z(k))

    blocks = [[0], [-1, 1], [-2, 2], [-3, 3], [4]]
    number = {0: 0, -1: 1, 1: 2, -2: 3, 2: 4, -3: 5, 3: 6, 4: 7}

    def z_of(o):
        return lax.rem(z + o + NZ, NZ)

    def to_slots(n, ref, table_of, out, whole):
        wait(ref.at[pl.ds(0, NY - 1)], y_recv.at[n + 1])
        rows = dot(table_of, ref[...].reshape(128, HALF), ROWS_T).astype(BF16)
        out[:, :, 0:HALF] = rows[0:64].reshape(NX, 16, HALF)
        out[:, :, HALF:WIDTH] = rows[64:128].reshape(NX, 16, HALF)
        for k in range(1, NX):
            there = lax.rem(x + k, NX)
            send(out.at[there], whole.at[z, c, x], x_send.at[n], x_recv.at[n], at_x(k))
        whole[z, c, x] = out[x]

    def ring(n, whole, s):
        for o in blocks[s]:
            ways = []
            if s == 0:
                wait(xs.at[pl.ds(0, NX - 1)], x_recv.at[n])
                ways = [0, 1]
            else:
                way = n if s == 4 else (0 if o < 0 else 1)
                here = whole.at[z_of(o), c]
                wait(here, ring_recv.at[n, way, s])
                if s < 3 or (s == 3 and way == n):
                    ways = [way]
            here = whole.at[z_of(o), c]
            for way in ways:
                send(here, here, ring_send.at[n, way, s], ring_recv.at[n, way, s + 1],
                     at_z(1 if way == 0 else -1))
            b = number[o]
            send(here, here, sib_send.at[n, b], sib_recv.at[n, b], sibling)

    def compute(o):
        b, zb = number[o], z_of(o)
        wait(xall.at[zb, 1 - c], sib_recv.at[0, b])
        wait(gall.at[zb, 1 - c], sib_recv.at[1, b])
        rows = xall[zb].reshape(128, WIDTH)
        scaled = gall[zb].reshape(128, WIDTH)
        pre = dot(rows, wgu[...])
        grad_hidden = dot(scaled, wd[...], COLS_T)
        gate_pre, up_pre = pre[:, :UNITS], pre[:, UNITS:]
        logistic = jax.nn.sigmoid(gate_pre)
        activated = gate_pre * logistic
        hi[zb] = (activated * up_pre).astype(BF16)
        grad_up = (grad_hidden * activated).astype(BF16)
        grad_gate = (
            grad_hidden * up_pre * (logistic * (1.0 + gate_pre * (1.0 - logistic)))
        ).astype(BF16)
        both = jnp.concatenate([grad_gate, grad_up], axis=1)
        hg[zb] = both
        pb[zb] = dot(both, wgu[...], COLS_T).astype(BF16).reshape(2, 64, WIDTH)
        send(pb.at[zb, 1 - c], pr.at[zb], p_send.at[b], p_recv.at[b], sibling)

    def pair_sum(o):
        b, zb = number[o], z_of(o)
        wait(pr.at[zb], p_recv.at[b])
        total = pb[zb, c].astype(F32) + pr[zb].astype(F32)
        qs[zb] = total.astype(BF16).reshape(NX, 16, WIDTH)
        for k in range(1, NX):
            there = lax.rem(x + k, NX)
            send(qs.at[zb, there], qr.at[zb, x], q_send.at[b], q_recv.at[b], at_x(k))
        qr[zb, x] = qs[zb, x]

    def combine(o):
        b, zb = number[o], z_of(o)
        wait(qr.at[zb, pl.ds(0, NX - 1)], q_recv.at[b])
        slots = qr[zb].reshape(64, WIDTH)
        halves = jnp.concatenate([slots[:, :HALF], slots[:, HALF:]], axis=0)
        ts[zb] = dot(szall[zb], halves).astype(BF16).reshape(NY, 16, HALF)
        for k in range(1, NY):
            there = lax.rem(y + k, NY)
            send(ts.at[zb, there], tr.at[zb, y], t_send.at[b], t_recv.at[b], at_y(k))
        tr[zb, y] = ts[zb, y]

    def y_sum(o):
        b, zb = number[o], z_of(o)
        wait(tr.at[zb, pl.ds(0, NY - 1)], t_recv.at[b])
        total = tr[zb, 0].astype(F32)
        for k in range(1, NY):
            total = total + tr[zb, k].astype(F32)
        fs[zb] = total.astype(BF16)
        if o == 0:
            fr[z] = fs[z]
        else:
            send(fs.at[zb], fr.at[z], f_send, f_recv, at_z(o))

    def weight_grads(first, last):
        def step(j, carry):
            at = pl.ds(pl.multiple_of(j * 256, 256), 256)
            both = hg[...].reshape(1024, 2 * UNITS)
            part = dot(xall[:, :, :, :, at].reshape(1024, 256), both, ROWS_T)
            gwg[0, at, :] = part[:, :UNITS]
            gwu[0, at, :] = part[:, UNITS:]
            hidden = hi[...].reshape(1024, UNITS)
            gwd[0, :, at] = dot(hidden, gall[:, :, :, :, at].reshape(1024, 256), ROWS_T)
            return carry

        lax.fori_loop(first, last, step, 0)

    to_slots(0, tyx, member, xs, xall)
    to_slots(1, tyg, weighted, gs, gall)
    ring(0, xall, 0)
    ring(1, gall, 0)
    for load in loads:
        load.wait()
    compute(0)
    wait(szall.at[pl.ds(0, NZ - 1)], i_recv)
    for s in range(1, 5):
        ring(0, xall, s)
        for o in blocks[s - 1]:
            pair_sum(o)
        for o in blocks[s - 1]:
            combine(o)
        ring(1, gall, s)
        for o in blocks[s]:
            compute(o)
        if s >= 2:
            for o in blocks[s - 2]:
                y_sum(o)
    weight_grads(0, 2)
    pair_sum(4)
    weight_grads(2, 4)
    combine(4)
    for o in blocks[3]:
        y_sum(o)
    weight_grads(4, 8)
    y_sum(4)
    wait(fr.at[pl.ds(0, NZ - 1)], f_recv)
    total = fr[0].astype(F32)
    for k in range(1, NZ):
        total = total + fr[k].astype(F32)
    gtok[:, 0:HALF] = total[0:8].astype(BF16)
    gtok[:, HALF:WIDTH] = total[8:16].astype(BF16)

    for n, ref in enumerate((inf, tyx, tyg)):
        wait(ref.at[pl.ds(0, NY - 1)], y_send.at[n])
    wait(szall.at[pl.ds(0, NZ - 1)], i_send)
    for n, whole in enumerate((xall, gall)):
        wait(xs.at[pl.ds(0, NX - 1)], x_send.at[n])
        for way in range(2):
            for s in range(4 if way == n else 3):
                wait(whole.at[0, 0], ring_send.at[n, way, s])
        for b in range(8):
            wait(whole.at[0, 0], sib_send.at[n, b])
    for b in range(8):
        wait(pr.at[0], p_send.at[b])
        wait(qs.at[0, pl.ds(0, NX - 1)], q_send.at[b])
        wait(ts.at[0, pl.ds(0, NY - 1)], t_send.at[b])
    wait(fs.at[pl.ds(0, NZ - 1)], f_send)


def on_device(tokens, grad_out, gate_weights, expert_ids, w_gate, w_up, w_down):
    vmem = pl.BlockSpec(memory_space=pltpu.VMEM)
    hbm = pl.BlockSpec(memory_space=pl.ANY)
    dma = pltpu.SemaphoreType.DMA
    rows = (NZ, 2, NX, 16, WIDTH)
    scratch = [
        pltpu.VMEM((WIDTH, 2 * UNITS), BF16),
        pltpu.VMEM((UNITS, WIDTH), BF16),
        pltpu.VMEM((NY, 16, 128), BF16),
        pltpu.VMEM((NY, 16, HALF), BF16),
        pltpu.VMEM((NY, 16, HALF), BF16),
        pltpu.VMEM((NX, 16, WIDTH), BF16),
        pltpu.VMEM((NX, 16, WIDTH), BF16),
        pltpu.VMEM(rows, BF16),
        pltpu.VMEM(rows, BF16),
        pltpu.VMEM((NZ, 128, 128), BF16),
        pltpu.VMEM((NZ, 128, 2 * UNITS), BF16),
        pltpu.VMEM((NZ, 128, UNITS), BF16),
        pltpu.VMEM((NZ, 2, 64, WIDTH), BF16),
        pltpu.VMEM((NZ, 64, WIDTH), BF16),
        pltpu.VMEM((NZ, NX, 16, WIDTH), BF16),
        pltpu.VMEM((NZ, NX, 16, WIDTH), BF16),
        pltpu.VMEM((NZ, NY, 16, HALF), BF16),
        pltpu.VMEM((NZ, NY, 16, HALF), BF16),
        pltpu.VMEM((NZ, 16, HALF), BF16),
        pltpu.VMEM((NZ, 16, HALF), BF16),
        dma((3,)),
        dma((3,)),
        dma((3,)),
        dma((2,)),
        dma((2,)),
        dma(()),
        dma(()),
        dma((2, 2, 4)),
        dma((2, 2, 5)),
        dma((2, 8)),
        dma((2, 8)),
        dma((8,)),
        dma((8,)),
        dma((8,)),
        dma((8,)),
        dma((8,)),
        dma((8,)),
        dma(()),
        dma(()),
    ]
    return pl.pallas_call(
        kernel,
        out_shape=(
            jax.ShapeDtypeStruct((8, WIDTH), BF16),
            jax.ShapeDtypeStruct((1, WIDTH, UNITS), F32),
            jax.ShapeDtypeStruct((1, WIDTH, UNITS), F32),
            jax.ShapeDtypeStruct((1, UNITS, WIDTH), F32),
        ),
        in_specs=[vmem, vmem, vmem, vmem, hbm, hbm, hbm],
        out_specs=(vmem, vmem, vmem, vmem),
        scratch_shapes=scratch,
        compiler_params=pltpu.CompilerParams(
            collective_id=0, has_side_effects=True, vmem_limit_bytes=56 * 2**20
        ),
        cost_estimate=pl.CostEstimate(
            flops=4_400_000_000, bytes_accessed=5_000_000, transcendentals=131072
        ),
    )(tokens, grad_out, gate_weights, expert_ids, w_gate, w_up, w_down)


def solution(mesh):
    placed = P(("dp", "expert"), None)
    columns, rows = P("expert", None, "dp"), P("expert", "dp", None)
    return jax.shard_map(
        on_device,
        mesh=mesh,
        in_specs=(placed, placed, placed, placed, columns, columns, rows),
        out_specs=(placed, columns, columns, rows),
        check_vma=False,
    )
```

```python
import jax
import jax.numpy as jnp
from jax import lax
from jax.experimental import pallas as pl
from jax.experimental.pallas import tpu as pltpu
from jax.sharding import PartitionSpec as P

NZ, NY, NX = 8, 8, 4
WIDTH, UNITS = 2048, 128
HALF = WIDTH // 2
F32, BF16 = jnp.float32, jnp.bfloat16
ROWS_T = (((0,), (0,)), ((), ()))
COLS_T = (((1,), (1,)), ((), ()))


def dot(a, b, dims=(((1,), (0,)), ((), ()))):
    return lax.dot_general(a, b, dims, preferred_element_type=F32)


def kernel(
    tok, gout, gw, ids, wg_hbm, wu_hbm, wd_hbm,
    gtok, gwg_hbm, gwu_hbm, gwd_hbm,
    gwg, gwu, gwd, wgu, wd, inf, tyx, tyg, xs, gs, xall, gall, szall, hg, hi, pb, pr, qs, qr, ts, tm, tn, tr, fs, fr,
    w_sem, o_sem, y_send, y_recv, x_send, x_recv, i_send, i_recv, ring_send, ring_recv,
    sib_send, sib_recv, p_send, p_recv, q_send, q_recv, m_send, m_recv, t_send, t_recv, f_send, f_recv,
):
    dp, ex = lax.axis_index("dp"), lax.axis_index("expert")
    z, c = dp // 2, lax.rem(dp, 2)
    y, x = ex // NX, lax.rem(ex, NX)

    def at_z(k):
        return {"dp": lax.rem(z + k + NZ, NZ) * 2 + c, "expert": ex}

    def at_y(k):
        return {"dp": dp, "expert": lax.rem(y + k + NY, NY) * NX + x}

    way = 1 - 2 * c

    def y_of(k):
        return lax.rem(y + way * k + NY, NY)

    def at_x(k):
        return {"dp": dp, "expert": y * NX + lax.rem(x + k, NX)}

    sibling = {"dp": z * 2 + 1 - c, "expert": ex}

    def send(src, dst, ssem, rsem, where):
        copy = pltpu.make_async_remote_copy(
            src_ref=src, dst_ref=dst, send_sem=ssem, recv_sem=rsem,
            device_id=where, device_id_type=pl.DeviceIdType.MESH,
        )
        copy.start()

    def wait(ref, sem):
        pltpu.make_async_copy(ref, ref, sem).wait()

    loads = [
        pltpu.make_async_copy(wg_hbm.at[0], wgu.at[:, pl.ds(0, UNITS)], w_sem.at[0]),
        pltpu.make_async_copy(wu_hbm.at[0], wgu.at[:, pl.ds(UNITS, UNITS)], w_sem.at[1]),
        pltpu.make_async_copy(wd_hbm.at[0], wd, w_sem.at[2]),
    ]
    for load in loads:
        load.start()

    barrier = pltpu.get_barrier_semaphore()
    partners = [at_y(k) for k in range(1, NY)] + [at_x(k) for k in range(1, NX)]
    partners += [at_z(k) for k in range(1, NZ)] + [sibling]
    for partner in partners:
        pl.semaphore_signal(barrier, inc=1, device_id=partner, device_id_type=pl.DeviceIdType.MESH)

    lane = lax.broadcasted_iota(jnp.int32, (8, 128), 1)
    eye = lax.broadcasted_iota(jnp.int32, (8, 8), 0) == lax.broadcasted_iota(jnp.int32, (8, 8), 1)
    ids32, gw32 = ids[...].astype(F32), gw[...].astype(F32)
    info = jnp.zeros((8, 128), F32)
    for n, part in enumerate((ids32, gw32)):
        for k in range(4):
            spread = jnp.where(eye, jnp.broadcast_to(part[k : k + 1, :], (8, 8)), 0.0)
            column = jnp.sum(spread, axis=1, keepdims=True)
            info = info + jnp.where(lane == 4 * n + k, column, 0.0)
    inf[y] = jnp.concatenate([info, info], axis=0).astype(BF16)
    t32 = tok[...].astype(F32)
    tyx[y] = jnp.concatenate([t32[:, :HALF], t32[:, HALF:]], axis=0).astype(BF16)
    g32 = gout[...].astype(F32)
    tyg[y] = jnp.concatenate([g32[:, :HALF], g32[:, HALF:]], axis=0).astype(BF16)

    pl.semaphore_wait(barrier, len(partners))

    def spread_y(n, ref):
        for k in range(1, NY):
            send(ref.at[y], ref.at[y], y_send.at[n], y_recv.at[n], at_y(k))

    spread_y(0, inf)
    spread_y(1, tyx)

    wait(inf.at[pl.ds(0, NY - 1)], y_recv.at[0])
    table = inf[...].reshape(128, 128).astype(F32)
    r = lax.broadcasted_iota(jnp.int32, (128, 128), 0)
    l = lax.broadcasted_iota(jnp.int32, (128, 128), 1)
    same = ((r // 8) % 2 == l // 64) & (r // 16 == (l // 2) % 8)
    expert = (y * NX + (l // 16) % 4).astype(F32)
    named = jnp.zeros((128, 128), F32)
    weight = jnp.zeros((128, 128), F32)
    for k in range(4):
        match = jnp.where(same & (table[:, k : k + 1] == expert), 1.0, 0.0)
        named = named + match
        weight = weight + match * table[:, 4 + k : 5 + k]
    before = jnp.where((r // 8 == l // 8) & (l < r), 1.0, 0.0).astype(BF16)
    rank = dot(before, named.astype(BF16))
    chosen = jnp.where(rank == (l % 2).astype(F32), named, 0.0)
    member = chosen.astype(BF16)
    weighted = (chosen * weight).astype(BF16)
    szall[z] = member
    for k in range(1, NZ):
        send(szall.at[z], szall.at[z], i_send, i_recv, at_z(k))

    blocks = [[0], [-1, 1], [-2, 2], [-3, 3], [4]]
    number = {0: 0, -1: 1, 1: 2, -2: 3, 2: 4, -3: 5, 3: 6, 4: 7}

    def z_of(o):
        return lax.rem(z + o + NZ, NZ)

    def to_slots(n, ref, table_of, out, whole):
        wait(ref.at[pl.ds(0, NY - 1)], y_recv.at[n + 1])
        if n == 0:
            spread_y(2, tyg)
        rows = dot(table_of, ref[...].reshape(128, HALF), ROWS_T).astype(BF16)
        out[:, :, 0:HALF] = rows[0:64].reshape(NX, 16, HALF)
        out[:, :, HALF:WIDTH] = rows[64:128].reshape(NX, 16, HALF)
        for k in range(1, NX):
            there = lax.rem(x + k, NX)
            send(out.at[there], whole.at[z, c, x], x_send.at[n], x_recv.at[n], at_x(k))
        whole[z, c, x] = out[x]

    def ring(n, whole, s):
        for o in blocks[s]:
            turns = []
            if s == 0:
                wait(xs.at[pl.ds(0, NX - 1)], x_recv.at[n])
                turns = [0, 1]
            else:
                turn = n if s == 4 else (0 if o < 0 else 1)
                here = whole.at[z_of(o), c]
                wait(here, ring_recv.at[n, turn, s])
                if s < 3 or (s == 3 and turn == n):
                    turns = [turn]
            here = whole.at[z_of(o), c]
            for turn in turns:
                send(here, here, ring_send.at[n, turn, s], ring_recv.at[n, turn, s + 1],
                     at_z(1 if turn == 0 else -1))
            b = number[o]
            send(here, here, sib_send.at[n, b], sib_recv.at[n, b], sibling)

    def compute(o):
        b, zb = number[o], z_of(o)
        wait(xall.at[zb, 1 - c], sib_recv.at[0, b])
        wait(gall.at[zb, 1 - c], sib_recv.at[1, b])
        rows = xall[zb].reshape(128, WIDTH)
        scaled = gall[zb].reshape(128, WIDTH)
        pre = dot(rows, wgu[...])
        grad_hidden = dot(scaled, wd[...], COLS_T)
        gate_pre, up_pre = pre[:, :UNITS], pre[:, UNITS:]
        logistic = jax.nn.sigmoid(gate_pre)
        activated = gate_pre * logistic
        hi[zb] = (activated * up_pre).astype(BF16)
        grad_up = (grad_hidden * activated).astype(BF16)
        grad_gate = (
            grad_hidden * up_pre * (logistic * (1.0 + gate_pre * (1.0 - logistic)))
        ).astype(BF16)
        both = jnp.concatenate([grad_gate, grad_up], axis=1)
        hg[zb] = both
        pb[zb] = dot(both, wgu[...], COLS_T).astype(BF16).reshape(2, 64, WIDTH)
        send(pb.at[zb, 1 - c], pr.at[zb], p_send.at[b], p_recv.at[b], sibling)

    def pair_sum(o):
        b, zb = number[o], z_of(o)
        wait(pr.at[zb], p_recv.at[b])
        total = pb[zb, c].astype(F32) + pr[zb].astype(F32)
        qs[zb] = total.astype(BF16).reshape(NX, 16, WIDTH)
        for k in range(1, NX):
            there = lax.rem(x + k, NX)
            send(qs.at[zb, there], qr.at[zb, x], q_send.at[b], q_recv.at[b], at_x(k))
        qr[zb, x] = qs[zb, x]

    def combine(o):
        b, zb = number[o], z_of(o)
        wait(qr.at[zb, pl.ds(0, NX - 1)], q_recv.at[b])
        slots = qr[zb].reshape(64, WIDTH)
        halves = jnp.concatenate([slots[:, :HALF], slots[:, HALF:]], axis=0)
        ts[zb] = dot(szall[zb], halves).astype(BF16).reshape(NY, 16, HALF)
        send(ts.at[zb, y_of(-3)], tm.at[zb, 0], m_send.at[b], m_recv.at[b], at_y(-way))
        send(ts.at[zb, y_of(-4)], tm.at[zb, 1], m_send.at[b], m_recv.at[b], at_y(way))
        send(ts.at[zb, y_of(-6)], tm.at[zb, 2], m_send.at[b], m_recv.at[b], at_y(way))
        send(ts.at[zb, y_of(-1)], tr.at[zb, 1], t_send.at[b], t_recv.at[b], at_y(-way))
        tr[zb, 0] = ts[zb, y]

    def merge(o):
        b, zb = number[o], z_of(o)
        wait(tm.at[zb], m_recv.at[b])
        for n, k in enumerate((2, 5, 7)):
            there = y_of(-k)
            total = ts[zb, there].astype(F32) + tm[zb, n].astype(F32)
            tn[zb, n] = total.astype(BF16)
            send(tn.at[zb, n], tr.at[zb, 2 + n], t_send.at[b], t_recv.at[b], at_y(-way * k))

    def y_sum(o):
        b, zb = number[o], z_of(o)
        wait(tr.at[zb, pl.ds(0, 4)], t_recv.at[b])
        total = tr[zb, 0].astype(F32)
        for k in range(1, 5):
            total = total + tr[zb, k].astype(F32)
        fs[zb] = total.astype(BF16)
        if o == 0:
            fr[z] = fs[z]
        else:
            send(fs.at[zb], fr.at[z], f_send, f_recv, at_z(o))

    def weight_grads(first, last):
        def step(j, carry):
            at = pl.ds(pl.multiple_of(j * 256, 256), 256)
            both = hg[...].reshape(1024, 2 * UNITS)
            part = dot(xall[:, :, :, :, at].reshape(1024, 256), both, ROWS_T)
            gwg[0, at, :] = part[:, :UNITS]
            gwu[0, at, :] = part[:, UNITS:]
            hidden = hi[...].reshape(1024, UNITS)
            gwd[0, :, at] = dot(hidden, gall[:, :, :, :, at].reshape(1024, 256), ROWS_T)
            pltpu.make_async_copy(gwg.at[0, at], gwg_hbm.at[0, at], o_sem.at[0]).start()
            pltpu.make_async_copy(gwu.at[0, at], gwu_hbm.at[0, at], o_sem.at[1]).start()
            pltpu.make_async_copy(gwd.at[0, :, at], gwd_hbm.at[0, :, at], o_sem.at[2]).start()
            return carry

        lax.fori_loop(first, last, step, 0)

    to_slots(0, tyx, member, xs, xall)
    ring(0, xall, 0)
    to_slots(1, tyg, weighted, gs, gall)
    ring(1, gall, 0)
    for load in loads:
        load.wait()
    compute(0)
    wait(szall.at[pl.ds(0, NZ - 1)], i_recv)
    for s in range(1, 5):
        ring(0, xall, s)
        for o in blocks[s - 1]:
            pair_sum(o)
        if s >= 2:
            for o in blocks[s - 2]:
                merge(o)
        ring(1, gall, s)
        if s < 4:
            for o in blocks[s - 1]:
                combine(o)
        for o in blocks[s]:
            compute(o)
        if s >= 2:
            for o in blocks[s - 2]:
                y_sum(o)
    for o in blocks[3]:
        combine(o)
    pair_sum(4)
    weight_grads(0, 2)
    for o in blocks[3]:
        merge(o)
    combine(4)
    weight_grads(2, 4)
    merge(4)
    for o in blocks[3]:
        y_sum(o)
    weight_grads(4, 7)
    y_sum(4)
    weight_grads(7, 8)
    wait(fr.at[pl.ds(0, NZ - 1)], f_recv)
    total = fr[0].astype(F32)
    for k in range(1, NZ):
        total = total + fr[k].astype(F32)
    gtok[:, 0:HALF] = total[0:8].astype(BF16)
    gtok[:, HALF:WIDTH] = total[8:16].astype(BF16)

    for n, ref in enumerate((inf, tyx, tyg)):
        wait(ref.at[pl.ds(0, NY - 1)], y_send.at[n])
    wait(szall.at[pl.ds(0, NZ - 1)], i_send)
    for n, whole in enumerate((xall, gall)):
        wait(xs.at[pl.ds(0, NX - 1)], x_send.at[n])
        for turn in range(2):
            for s in range(4 if turn == n else 3):
                wait(whole.at[0, 0], ring_send.at[n, turn, s])
        for b in range(8):
            wait(whole.at[0, 0], sib_send.at[n, b])
    for b in range(8):
        wait(pr.at[0], p_send.at[b])
        wait(qs.at[0, pl.ds(0, NX - 1)], q_send.at[b])
        wait(tm.at[0], m_send.at[b])
        wait(tr.at[0, pl.ds(0, 4)], t_send.at[b])
    wait(fs.at[pl.ds(0, NZ - 1)], f_send)
    for n, ref in enumerate((gwg, gwu, gwd)):
        wait(ref, o_sem.at[n])


def hand_over(tok, gate, up, down, tok_out, gate_out, up_out, down_out, *scratch):
    held, in_sem, out_sem = scratch[:4], scratch[4], scratch[5]
    pieces = []
    for k in range(4):
        for n, extent in ((1, WIDTH), (2, WIDTH), (3, UNITS)):
            pieces.append((n, (0, pl.ds(k * extent // 4, extent // 4))))
    pieces.append((0, (pl.ds(0, 8),)))
    ins, outs = (tok, gate, up, down), (tok_out, gate_out, up_out, down_out)
    loads, stores = [], []
    for m, (n, at) in enumerate(pieces):
        loads.append(pltpu.make_async_copy(ins[n].at[at], held[n].at[at], in_sem.at[m]))
        stores.append(pltpu.make_async_copy(held[n].at[at], outs[n].at[at], out_sem.at[m]))
    for load in loads:
        load.start()
    for load, store in zip(loads, stores):
        load.wait()
        store.start()
    for store in stores:
        store.wait()


def on_device(tokens, grad_out, gate_weights, expert_ids, w_gate, w_up, w_down):
    vmem = pl.BlockSpec(memory_space=pltpu.VMEM)
    hbm = pl.BlockSpec(memory_space=pl.ANY)
    dma = pltpu.SemaphoreType.DMA
    rows = (NZ, 2, NX, 16, WIDTH)
    scratch = [
        pltpu.VMEM((1, WIDTH, UNITS), F32),
        pltpu.VMEM((1, WIDTH, UNITS), F32),
        pltpu.VMEM((1, UNITS, WIDTH), F32),
        pltpu.VMEM((WIDTH, 2 * UNITS), BF16),
        pltpu.VMEM((UNITS, WIDTH), BF16),
        pltpu.VMEM((NY, 16, 128), BF16),
        pltpu.VMEM((NY, 16, HALF), BF16),
        pltpu.VMEM((NY, 16, HALF), BF16),
        pltpu.VMEM((NX, 16, WIDTH), BF16),
        pltpu.VMEM((NX, 16, WIDTH), BF16),
        pltpu.VMEM(rows, BF16),
        pltpu.VMEM(rows, BF16),
        pltpu.VMEM((NZ, 128, 128), BF16),
        pltpu.VMEM((NZ, 128, 2 * UNITS), BF16),
        pltpu.VMEM((NZ, 128, UNITS), BF16),
        pltpu.VMEM((NZ, 2, 64, WIDTH), BF16),
        pltpu.VMEM((NZ, 64, WIDTH), BF16),
        pltpu.VMEM((NZ, NX, 16, WIDTH), BF16),
        pltpu.VMEM((NZ, NX, 16, WIDTH), BF16),
        pltpu.VMEM((NZ, NY, 16, HALF), BF16),
        pltpu.VMEM((NZ, 3, 16, HALF), BF16),
        pltpu.VMEM((NZ, 3, 16, HALF), BF16),
        pltpu.VMEM((NZ, 5, 16, HALF), BF16),
        pltpu.VMEM((NZ, 16, HALF), BF16),
        pltpu.VMEM((NZ, 16, HALF), BF16),
        dma((3,)),
        dma((3,)),
        dma((3,)),
        dma((3,)),
        dma((2,)),
        dma((2,)),
        dma(()),
        dma(()),
        dma((2, 2, 4)),
        dma((2, 2, 5)),
        dma((2, 8)),
        dma((2, 8)),
        dma((8,)),
        dma((8,)),
        dma((8,)),
        dma((8,)),
        dma((8,)),
        dma((8,)),
        dma((8,)),
        dma((8,)),
        dma(()),
        dma(()),
    ]
    outs = pl.pallas_call(
        kernel,
        out_shape=(
            jax.ShapeDtypeStruct((8, WIDTH), BF16),
            jax.ShapeDtypeStruct((1, WIDTH, UNITS), F32),
            jax.ShapeDtypeStruct((1, WIDTH, UNITS), F32),
            jax.ShapeDtypeStruct((1, UNITS, WIDTH), F32),
        ),
        in_specs=[vmem, vmem, vmem, vmem, hbm, hbm, hbm],
        out_specs=(vmem, hbm, hbm, hbm),
        scratch_shapes=scratch,
        compiler_params=pltpu.CompilerParams(
            collective_id=0, has_side_effects=True, vmem_limit_bytes=56 * 2**20
        ),
        cost_estimate=pl.CostEstimate(
            flops=4_400_000_000, bytes_accessed=5_000_000, transcendentals=131072
        ),
    )(tokens, grad_out, gate_weights.T, expert_ids.T, w_gate, w_up, w_down)
    return pl.pallas_call(
        hand_over,
        out_shape=tuple(jax.ShapeDtypeStruct(out.shape, out.dtype) for out in outs),
        in_specs=[hbm] * 4,
        out_specs=(hbm,) * 4,
        scratch_shapes=[pltpu.VMEM(out.shape, out.dtype) for out in outs] + [dma((13,)), dma((13,))],
        compiler_params=pltpu.CompilerParams(vmem_limit_bytes=56 * 2**20),
    )(*outs)


def solution(mesh):
    placed = P(("dp", "expert"), None)
    columns, rows = P("expert", None, "dp"), P("expert", "dp", None)
    return jax.shard_map(
        on_device,
        mesh=mesh,
        in_specs=(placed, placed, placed, placed, columns, columns, rows),
        out_specs=(placed, columns, columns, rows),
        check_vma=False,
    )
```

```python
import jax
import jax.numpy as jnp
from jax import lax
from jax.experimental import pallas as pl
from jax.experimental.pallas import tpu as pltpu
from jax.sharding import PartitionSpec as P

NZ, NY, NX = 8, 8, 4
WIDTH, UNITS = 2048, 128
HALF = WIDTH // 2
F32, BF16 = jnp.float32, jnp.bfloat16
ROWS_T = (((0,), (0,)), ((), ()))


def dot(a, b, dims=(((1,), (0,)), ((), ()))):
    return lax.dot_general(a, b, dims, preferred_element_type=F32)


def kernel(
    tok, gout, gw, ids, wg_hbm, wu_hbm, wd_hbm,
    gtok, gwg_hbm, gwu_hbm, gwd_hbm,
    gwg, gwu, gwd, wgu, wd, wgu_t, wd_t, inf, tyx, tyg, xs, gs, xall, gall, szall, hg, hi, pb, pr, qs, qr, ts, tm, tn, tr, last, fs, fr,
    w_sem, o_sem, y_send, y_recv, x_send, x_recv, i_send, i_recv, ring_send, ring_recv,
    sib_send, sib_recv, p_send, p_recv, q_send, q_recv, m_send, m_recv, t_send, t_recv, f_send, f_recv,
):
    dp, ex = lax.axis_index("dp"), lax.axis_index("expert")
    z, c = dp // 2, lax.rem(dp, 2)
    y, x = ex // NX, lax.rem(ex, NX)

    def at_z(k):
        return {"dp": lax.rem(z + k + NZ, NZ) * 2 + c, "expert": ex}

    def at_y(k):
        return {"dp": dp, "expert": lax.rem(y + k + NY, NY) * NX + x}

    way = 1 - 2 * c

    def y_of(k):
        return lax.rem(y + way * k + NY, NY)

    def at_x(k):
        return {"dp": dp, "expert": y * NX + lax.rem(x + k, NX)}

    sibling = {"dp": z * 2 + 1 - c, "expert": ex}

    def send(src, dst, ssem, rsem, where):
        copy = pltpu.make_async_remote_copy(
            src_ref=src, dst_ref=dst, send_sem=ssem, recv_sem=rsem,
            device_id=where, device_id_type=pl.DeviceIdType.MESH,
        )
        copy.start()

    def wait(ref, sem):
        pltpu.make_async_copy(ref, ref, sem).wait()

    loads = [
        pltpu.make_async_copy(wg_hbm.at[0], wgu.at[:, pl.ds(0, UNITS)], w_sem.at[0]),
        pltpu.make_async_copy(wu_hbm.at[0], wgu.at[:, pl.ds(UNITS, UNITS)], w_sem.at[1]),
        pltpu.make_async_copy(wd_hbm.at[0], wd, w_sem.at[2]),
    ]
    for load in loads:
        load.start()

    barrier = pltpu.get_barrier_semaphore()
    partners = [at_y(k) for k in range(1, NY)] + [at_x(k) for k in range(1, NX)]
    partners += [at_z(k) for k in range(1, NZ)] + [sibling]
    for partner in partners:
        pl.semaphore_signal(barrier, inc=1, device_id=partner, device_id_type=pl.DeviceIdType.MESH)

    lane = lax.broadcasted_iota(jnp.int32, (8, 128), 1)
    eye = lax.broadcasted_iota(jnp.int32, (8, 8), 0) == lax.broadcasted_iota(jnp.int32, (8, 8), 1)
    ids32, gw32 = ids[...].astype(F32), gw[...].astype(F32)
    info = jnp.zeros((8, 128), F32)
    for n, part in enumerate((ids32, gw32)):
        for k in range(4):
            spread = jnp.where(eye, jnp.broadcast_to(part[k : k + 1, :], (8, 8)), 0.0)
            column = jnp.sum(spread, axis=1, keepdims=True)
            info = info + jnp.where(lane == 4 * n + k, column, 0.0)
    inf[y] = jnp.concatenate([info, info], axis=0).astype(BF16)
    t32 = tok[...].astype(F32)
    tyx[y] = jnp.concatenate([t32[:, :HALF], t32[:, HALF:]], axis=0).astype(BF16)
    g32 = gout[...].astype(F32)
    tyg[y] = jnp.concatenate([g32[:, :HALF], g32[:, HALF:]], axis=0).astype(BF16)

    pl.semaphore_wait(barrier, len(partners))

    def spread_y(n, ref):
        for k in range(1, NY):
            send(ref.at[y], ref.at[y], y_send.at[n], y_recv.at[n], at_y(k))

    spread_y(0, inf)
    spread_y(1, tyx)

    wait(inf.at[pl.ds(0, NY - 1)], y_recv.at[0])
    table = inf[...].reshape(128, 128).astype(F32)
    r = lax.broadcasted_iota(jnp.int32, (128, 128), 0)
    l = lax.broadcasted_iota(jnp.int32, (128, 128), 1)
    same = ((r // 8) % 2 == l // 64) & (r // 16 == (l // 2) % 8)
    expert = (y * NX + (l // 16) % 4).astype(F32)
    named = jnp.zeros((128, 128), F32)
    weight = jnp.zeros((128, 128), F32)
    for k in range(4):
        match = jnp.where(same & (table[:, k : k + 1] == expert), 1.0, 0.0)
        named = named + match
        weight = weight + match * table[:, 4 + k : 5 + k]
    before = jnp.where((r // 8 == l // 8) & (l < r), 1.0, 0.0).astype(BF16)
    rank = dot(before, named.astype(BF16))
    chosen = jnp.where(rank == (l % 2).astype(F32), named, 0.0)
    member = chosen.astype(BF16)
    weighted = (chosen * weight).astype(BF16)
    szall[z] = member
    for k in range(1, NZ):
        send(szall.at[z], szall.at[z], i_send, i_recv, at_z(k))

    for load in loads:
        load.wait()
    wgu_t[...] = wgu[...].T
    wd_t[...] = wd[...].T

    blocks = [[0], [-1, 1], [-2, 2], [-3, 3], [4]]
    number = {0: 0, -1: 1, 1: 2, -2: 3, 2: 4, -3: 5, 3: 6, 4: 7}

    def z_of(o):
        return lax.rem(z + o + NZ, NZ)

    def to_slots(n, ref, table_of, out, whole):
        wait(ref.at[pl.ds(0, NY - 1)], y_recv.at[n + 1])
        if n == 0:
            spread_y(2, tyg)
        rows = dot(table_of, ref[...].reshape(128, HALF), ROWS_T).astype(BF16)
        out[:, :, 0:HALF] = rows[0:64].reshape(NX, 16, HALF)
        out[:, :, HALF:WIDTH] = rows[64:128].reshape(NX, 16, HALF)
        for k in range(1, NX):
            there = lax.rem(x + k, NX)
            send(out.at[there], whole.at[z, c, x], x_send.at[n], x_recv.at[n], at_x(k))
        whole[z, c, x] = out[x]

    def ring(n, whole, s):
        for o in blocks[s]:
            turns = []
            if s == 0:
                wait(xs.at[pl.ds(0, NX - 1)], x_recv.at[n])
                turns = [0, 1]
            else:
                turn = n if s == 4 else (0 if o < 0 else 1)
                here = whole.at[z_of(o), c]
                wait(here, ring_recv.at[n, turn, s])
                if s < 3 or (s == 3 and turn == n):
                    turns = [turn]
            here = whole.at[z_of(o), c]
            for turn in turns:
                send(here, here, ring_send.at[n, turn, s], ring_recv.at[n, turn, s + 1],
                     at_z(1 if turn == 0 else -1))
            b = number[o]
            send(here, here, sib_send.at[n, b], sib_recv.at[n, b], sibling)

    def compute(o):
        b, zb = number[o], z_of(o)
        wait(xall.at[zb, 1 - c], sib_recv.at[0, b])
        wait(gall.at[zb, 1 - c], sib_recv.at[1, b])
        rows = xall[zb].reshape(128, WIDTH)
        scaled = gall[zb].reshape(128, WIDTH)
        pre = dot(rows, wgu[...])
        grad_hidden = dot(scaled, wd_t[...])
        gate_pre, up_pre = pre[:, :UNITS], pre[:, UNITS:]
        logistic = jax.nn.sigmoid(gate_pre)
        activated = gate_pre * logistic
        hi[zb] = (activated * up_pre).astype(BF16)
        grad_up = (grad_hidden * activated).astype(BF16)
        grad_gate = (
            grad_hidden * up_pre * (logistic * (1.0 + gate_pre * (1.0 - logistic)))
        ).astype(BF16)
        both = jnp.concatenate([grad_gate, grad_up], axis=1)
        hg[zb] = both
        pb[zb] = dot(both, wgu_t[...]).astype(BF16).reshape(2, 64, WIDTH)
        send(pb.at[zb, 1 - c], pr.at[zb], p_send.at[b], p_recv.at[b], sibling)

    def pair_sum(o):
        b, zb = number[o], z_of(o)
        wait(pr.at[zb], p_recv.at[b])
        total = pb[zb, c].astype(F32) + pr[zb].astype(F32)
        qs[zb] = total.astype(BF16).reshape(NX, 16, WIDTH)
        for k in range(1, NX):
            there = lax.rem(x + k, NX)
            send(qs.at[zb, there], qr.at[zb, x], q_send.at[b], q_recv.at[b], at_x(k))
        qr[zb, x] = qs[zb, x]

    def combine(o):
        b, zb = number[o], z_of(o)
        wait(qr.at[zb, pl.ds(0, NX - 1)], q_recv.at[b])
        slots = qr[zb].reshape(64, WIDTH)
        halves = jnp.concatenate([slots[:, :HALF], slots[:, HALF:]], axis=0)
        ts[zb] = dot(szall[zb], halves).astype(BF16).reshape(NY, 16, HALF)
        if o == 4:
            for k in range(1, NY):
                there = lax.rem(y + k, NY)
                send(ts.at[zb, there], last.at[y], t_send.at[b], t_recv.at[b], at_y(k))
            last[y] = ts[zb, y]
            return
        send(ts.at[zb, y_of(-3)], tm.at[zb, 0], m_send.at[b], m_recv.at[b], at_y(-way))
        send(ts.at[zb, y_of(-4)], tm.at[zb, 1], m_send.at[b], m_recv.at[b], at_y(way))
        send(ts.at[zb, y_of(-6)], tm.at[zb, 2], m_send.at[b], m_recv.at[b], at_y(way))
        send(ts.at[zb, y_of(-1)], tr.at[zb, 1], t_send.at[b], t_recv.at[b], at_y(-way))
        tr[zb, 0] = ts[zb, y]

    def merge(o):
        b, zb = number[o], z_of(o)
        wait(tm.at[zb], m_recv.at[b])
        for n, k in enumerate((2, 5, 7)):
            there = y_of(-k)
            total = ts[zb, there].astype(F32) + tm[zb, n].astype(F32)
            tn[zb, n] = total.astype(BF16)
            send(tn.at[zb, n], tr.at[zb, 2 + n], t_send.at[b], t_recv.at[b], at_y(-way * k))

    def y_sum(o):
        b, zb = number[o], z_of(o)
        parts = last if o == 4 else tr.at[zb]
        count = parts.shape[0]
        wait(parts.at[pl.ds(0, count - 1)], t_recv.at[b])
        total = parts[0].astype(F32)
        for k in range(1, count):
            total = total + parts[k].astype(F32)
        fs[zb] = total.astype(BF16)
        if o == 0:
            fr[z] = fs[z]
        else:
            send(fs.at[zb], fr.at[z], f_send, f_recv, at_z(o))

    def weight_grads(first, last):
        def step(j, carry):
            at = pl.ds(pl.multiple_of(j * 256, 256), 256)
            both = hg[...].reshape(1024, 2 * UNITS)
            part = dot(xall[:, :, :, :, at].reshape(1024, 256), both, ROWS_T)
            gwg[0, at, :] = part[:, :UNITS]
            gwu[0, at, :] = part[:, UNITS:]
            hidden = hi[...].reshape(1024, UNITS)
            gwd[0, :, at] = dot(hidden, gall[:, :, :, :, at].reshape(1024, 256), ROWS_T)
            pltpu.make_async_copy(gwg.at[0, at], gwg_hbm.at[0, at], o_sem.at[0]).start()
            pltpu.make_async_copy(gwu.at[0, at], gwu_hbm.at[0, at], o_sem.at[1]).start()
            pltpu.make_async_copy(gwd.at[0, :, at], gwd_hbm.at[0, :, at], o_sem.at[2]).start()
            return carry

        lax.fori_loop(first, last, step, 0)

    to_slots(0, tyx, member, xs, xall)
    ring(0, xall, 0)
    to_slots(1, tyg, weighted, gs, gall)
    ring(1, gall, 0)
    compute(0)
    wait(szall.at[pl.ds(0, NZ - 1)], i_recv)
    for s in range(1, 5):
        ring(0, xall, s)
        for o in blocks[s - 1]:
            pair_sum(o)
        if s >= 2:
            for o in blocks[s - 2]:
                merge(o)
        ring(1, gall, s)
        for o in blocks[s]:
            compute(o)
        for o in blocks[s - 1]:
            combine(o)
        if s >= 2:
            for o in blocks[s - 2]:
                y_sum(o)
    pair_sum(4)
    weight_grads(0, 2)
    for o in blocks[3]:
        merge(o)
    combine(4)
    weight_grads(2, 4)
    for o in blocks[3]:
        y_sum(o)
    weight_grads(4, 7)
    for n, ref in enumerate((inf, tyx, tyg)):
        wait(ref.at[pl.ds(0, NY - 1)], y_send.at[n])
    wait(szall.at[pl.ds(0, NZ - 1)], i_send)
    for n, whole in enumerate((xall, gall)):
        wait(xs.at[pl.ds(0, NX - 1)], x_send.at[n])
        for turn in range(2):
            for s in range(4 if turn == n else 3):
                wait(whole.at[0, 0], ring_send.at[n, turn, s])
        for b in range(8):
            wait(whole.at[0, 0], sib_send.at[n, b])
    for b in range(8):
        wait(pr.at[0], p_send.at[b])
        wait(qs.at[0, pl.ds(0, NX - 1)], q_send.at[b])
        if b < 7:
            wait(tm.at[0], m_send.at[b])
    y_sum(4)
    weight_grads(7, 8)
    wait(fr.at[pl.ds(0, NZ - 1)], f_recv)
    total = fr[0].astype(F32)
    for k in range(1, NZ):
        total = total + fr[k].astype(F32)
    gtok[:, 0:HALF] = total[0:8].astype(BF16)
    gtok[:, HALF:WIDTH] = total[8:16].astype(BF16)

    for b in range(8):
        wait(last.at[pl.ds(0, 7)] if b == 7 else tr.at[0, pl.ds(0, 4)], t_send.at[b])
    wait(fs.at[pl.ds(0, NZ - 1)], f_send)
    for n, ref in enumerate((gwg, gwu, gwd)):
        wait(ref, o_sem.at[n])


def hand_over(tok, gate, up, down, tok_out, gate_out, up_out, down_out, *scratch):
    held, in_sem, out_sem = scratch[:4], scratch[4], scratch[5]
    pieces = []
    for k in range(4):
        for n, extent in ((1, WIDTH), (2, WIDTH), (3, UNITS)):
            pieces.append((n, (0, pl.ds(k * extent // 4, extent // 4))))
    pieces.append((0, (pl.ds(0, 8),)))
    ins, outs = (tok, gate, up, down), (tok_out, gate_out, up_out, down_out)
    loads, stores = [], []
    for m, (n, at) in enumerate(pieces):
        loads.append(pltpu.make_async_copy(ins[n].at[at], held[n].at[at], in_sem.at[m]))
        stores.append(pltpu.make_async_copy(held[n].at[at], outs[n].at[at], out_sem.at[m]))
    for load in loads:
        load.start()
    for load, store in zip(loads, stores):
        load.wait()
        store.start()
    for store in stores:
        store.wait()


def on_device(tokens, grad_out, gate_weights, expert_ids, w_gate, w_up, w_down):
    vmem = pl.BlockSpec(memory_space=pltpu.VMEM)
    hbm = pl.BlockSpec(memory_space=pl.ANY)
    dma = pltpu.SemaphoreType.DMA
    rows = (NZ, 2, NX, 16, WIDTH)
    scratch = [
        pltpu.VMEM((1, WIDTH, UNITS), F32),
        pltpu.VMEM((1, WIDTH, UNITS), F32),
        pltpu.VMEM((1, UNITS, WIDTH), F32),
        pltpu.VMEM((WIDTH, 2 * UNITS), BF16),
        pltpu.VMEM((UNITS, WIDTH), BF16),
        pltpu.VMEM((2 * UNITS, WIDTH), BF16),
        pltpu.VMEM((WIDTH, UNITS), BF16),
        pltpu.VMEM((NY, 16, 128), BF16),
        pltpu.VMEM((NY, 16, HALF), BF16),
        pltpu.VMEM((NY, 16, HALF), BF16),
        pltpu.VMEM((NX, 16, WIDTH), BF16),
        pltpu.VMEM((NX, 16, WIDTH), BF16),
        pltpu.VMEM(rows, BF16),
        pltpu.VMEM(rows, BF16),
        pltpu.VMEM((NZ, 128, 128), BF16),
        pltpu.VMEM((NZ, 128, 2 * UNITS), BF16),
        pltpu.VMEM((NZ, 128, UNITS), BF16),
        pltpu.VMEM((NZ, 2, 64, WIDTH), BF16),
        pltpu.VMEM((NZ, 64, WIDTH), BF16),
        pltpu.VMEM((NZ, NX, 16, WIDTH), BF16),
        pltpu.VMEM((NZ, NX, 16, WIDTH), BF16),
        pltpu.VMEM((NZ, NY, 16, HALF), BF16),
        pltpu.VMEM((NZ, 3, 16, HALF), BF16),
        pltpu.VMEM((NZ, 3, 16, HALF), BF16),
        pltpu.VMEM((NZ, 5, 16, HALF), BF16),
        pltpu.VMEM((NY, 16, HALF), BF16),
        pltpu.VMEM((NZ, 16, HALF), BF16),
        pltpu.VMEM((NZ, 16, HALF), BF16),
        dma((3,)),
        dma((3,)),
        dma((3,)),
        dma((3,)),
        dma((2,)),
        dma((2,)),
        dma(()),
        dma(()),
        dma((2, 2, 4)),
        dma((2, 2, 5)),
        dma((2, 8)),
        dma((2, 8)),
        dma((8,)),
        dma((8,)),
        dma((8,)),
        dma((8,)),
        dma((8,)),
        dma((8,)),
        dma((8,)),
        dma((8,)),
        dma(()),
        dma(()),
    ]
    outs = pl.pallas_call(
        kernel,
        out_shape=(
            jax.ShapeDtypeStruct((8, WIDTH), BF16),
            jax.ShapeDtypeStruct((1, WIDTH, UNITS), F32),
            jax.ShapeDtypeStruct((1, WIDTH, UNITS), F32),
            jax.ShapeDtypeStruct((1, UNITS, WIDTH), F32),
        ),
        in_specs=[vmem, vmem, vmem, vmem, hbm, hbm, hbm],
        out_specs=(vmem, hbm, hbm, hbm),
        scratch_shapes=scratch,
        compiler_params=pltpu.CompilerParams(
            collective_id=0, has_side_effects=True, vmem_limit_bytes=56 * 2**20
        ),
        cost_estimate=pl.CostEstimate(
            flops=4_400_000_000, bytes_accessed=5_000_000, transcendentals=131072
        ),
    )(tokens, grad_out, gate_weights.T, expert_ids.T, w_gate, w_up, w_down)
    return pl.pallas_call(
        hand_over,
        out_shape=tuple(jax.ShapeDtypeStruct(out.shape, out.dtype) for out in outs),
        in_specs=[hbm] * 4,
        out_specs=(hbm,) * 4,
        scratch_shapes=[pltpu.VMEM(out.shape, out.dtype) for out in outs] + [dma((13,)), dma((13,))],
        compiler_params=pltpu.CompilerParams(vmem_limit_bytes=56 * 2**20),
    )(*outs)


def solution(mesh):
    placed = P(("dp", "expert"), None)
    columns, rows = P("expert", None, "dp"), P("expert", "dp", None)
    return jax.shard_map(
        on_device,
        mesh=mesh,
        in_specs=(placed, placed, placed, placed, columns, columns, rows),
        out_specs=(placed, columns, columns, rows),
        check_vma=False,
    )
```
